128 devices in a mesh: feat: 8 (over y, core), ex: 16 (over z, x).
Axes of the slice: x: 4, y: 4, z: 4, core: 2. Of those that a mesh axis runs over, the one named last changes fastest.
Arguments:
- gradients: bfloat16 [16, 67108864], P('ex', 'feat'), may hold values from -6 to 6
- sign_words: int32 [4194304], P('feat'), may hold values from 0 to 65535
- sub_index: int32 [8192], replicated, may hold values from 0 to 67108863, as said below
- test_sketch: bfloat16 [1024, 8192], P('ex'), may hold values from -6 to 6
Outputs:
- scores: float32 [16, 1024], P('ex')
The draws below stay inside these ranges and needn't reach their ends.
Inputs may be any that keep to these rules, and one draw needn't show every extreme that they name: `sub_index`: strictly increasing; entry k lies in [k * 8192, (k + 1) * 8192); the first entry is 0 and the last is 67108863.
All inputs are finite; a program needn't handle non-finite values.
Results may differ from the reference program's by a relative error of at most 0.0051.
Values may be sent and summed in bfloat16 or wider, within the bound.
A program may use at most 640 MiB of HBM per device.

```python
import jax
import jax.numpy as jnp
from jax import lax

NHIGH = 1024
NMID = 256
NLOW = 256
K = 8192
TESTS = 1024
F = 67108864
EXAMPLES = 16


def draw_sub_index(key, part):
    stride = NHIGH * NMID * NLOW // K
    offsets = jax.random.randint(key, (K,), 0, stride, dtype=jnp.int32)
    offsets = offsets.at[0].set(0)
    offsets = offsets.at[K - 1].set(stride - 1)
    return jnp.arange(K, dtype=jnp.int32) * stride + offsets


def place_ends(drawn, key, least, largest):
    dims = drawn.shape
    spot = [jax.random.randint(jax.random.fold_in(key, axis), (), 0, dims[axis]) for axis in range(len(dims))]
    drawn = drawn.at[tuple(spot)].set(least)
    longest = dims.index(max(dims))
    spot[longest] = (spot[longest] + 1) % dims[longest]
    return drawn.at[tuple(spot)].set(largest)


def steps_of(own_key, shape, shards, low, top_value):
    level, own = 1.0, jax.random.fold_in(own_key, 6)
    for dim, shards_of in shards:
        draws = jnp.exp(jax.random.uniform(jax.random.fold_in(own, dim), (shards_of,), jnp.float32, low / len(shards), top_value / len(shards)))
        level = level * jnp.repeat(draws, shape[dim] // shards_of).reshape([-1 if axis == dim else 1 for axis in range(len(shape))])
    return level


def centred(own_key, extent, width, most, shards=(), kind=jnp.bfloat16):
    gain = steps_of(own_key, extent, shards, -0.22, 0.18) if shards else 1.0
    drawn = jax.random.normal(own_key, extent, jnp.float32) * width * gain
    return jnp.minimum(jnp.maximum(drawn, -most), most).astype(kind)


def setup_inputs(seed: int = 0) -> dict:
    key_list = jax.random.split(jax.random.key(seed), 5)
    return {
        "gradients": centred(key_list[0], (EXAMPLES, F), 1.0, 6.0, ((0, 16), (1, 8))),
        "sign_words": place_ends(jax.random.randint(key_list[1], (F // 16,), 0, 65536), jax.random.fold_in(key_list[1], 1), 0, 65535).astype(jnp.int32),
        "sub_index": draw_sub_index(jax.random.fold_in(key_list[4], 71), 0),
        "test_sketch": centred(key_list[3], (TESTS, K), 1.0, 6.0, ((0, 16),)),
    }


def parity_sign(left, right, nbits):
    common = jnp.bitwise_and(left, right)
    total = jnp.zeros_like(common)
    for position in range(nbits):
        total = total + jnp.bitwise_and(jnp.right_shift(common, position), 1)
    return (1 - 2 * (total % 2)).astype(jnp.float32)


def hadamard_table(order):
    places = jnp.arange(order, dtype=jnp.int32)
    return parity_sign(places[:, None], places[None, :], order.bit_length() - 1)


def reference(gradients, sign_words, sub_index, test_sketch):
    total_features = NHIGH * NMID * NLOW
    shifts = jnp.arange(16, dtype=jnp.int32)
    flags = jnp.bitwise_and(jnp.right_shift(sign_words.astype(jnp.int32)[:, None], shifts[None, :]), 1).reshape(total_features)
    signs = (2 * flags - 1).astype(jnp.bfloat16)
    low_table = hadamard_table(NLOW)
    mid_table = hadamard_table(NMID)
    high_of = (sub_index // (NMID * NLOW)).astype(jnp.int32)
    col_of = (sub_index % (NMID * NLOW)).astype(jnp.int32)
    rows = jnp.arange(NHIGH, dtype=jnp.int32)
    select = parity_sign(rows[:, None], high_of[None, :], NHIGH.bit_length() - 1)
    feature_scale = float(total_features) ** -0.5

    def one_example(grad):
        signed = (grad * signs).reshape(NHIGH, NMID, NLOW)
        first = jnp.einsum("hml,pl->hmp", signed.astype(jnp.float32), low_table).astype(jnp.bfloat16)
        second = jnp.einsum("hml,qm->hql", first.astype(jnp.float32), mid_table).astype(jnp.bfloat16)
        second = second.reshape(NHIGH, NMID * NLOW)
        picked = jnp.take(second, col_of, axis=1).astype(jnp.float32)
        return jnp.sum(select * picked, axis=0) * feature_scale

    sketch = lax.map(one_example, gradients)
    sketch_rounded = sketch.astype(jnp.bfloat16)
    scores = jnp.einsum("ek,tk->et", sketch_rounded.astype(jnp.float32), test_sketch.astype(jnp.float32))
    return scores * (float(K) ** -0.5)
```

```python
import jax, jax.numpy as jnp, numpy as np
from jax import lax
from jax.experimental import pallas as pl
from jax.experimental.pallas import tpu as pltpu
from jax.sharding import PartitionSpec as P

def hada(n):
    h=np.ones((1,1))
    while h.shape[0]<n: h=np.block([[h,h],[h,-h]])
    return h

def k1_matrix():
    h32, h8 = hada(32), hada(8)
    rows = np.zeros((256,256))
    for j in range(16):
        for t in range(16):
            h5 = j + 16*(t//8); s = t%8
            rows[:, 16*j+t] = np.kron(h32[:,h5], h8[:,s])
    return rows

FB = 16384
NBLK = 16
NS = 6
UPB = FB//2048

def kernel(g_ref, w_ref, km_ref, kp_ref, kq_ref, ks_ref, h4_ref, hm_ref, hb_ref, out_ref,
           raw, words, psel, sq, xs, ts, sem):
    def copies(b, slot):
        h2 = b // 4
        mb = b % 4
        return (pltpu.make_async_copy(g_ref.at[:, h2, :, pl.ds(mb*FB, FB)], raw.at[slot], sem.at[0, slot]),
                pltpu.make_async_copy(w_ref.at[:, h2, pl.ds(mb*8, 8), :], words.at[slot], sem.at[1, slot]))
    for b in range(NS):
        for c in copies(b, b): c.start()
    rows = lax.broadcasted_iota(jnp.int32, (256,256), 0)
    urow = lax.broadcasted_iota(jnp.int32, (32,256), 0)
    @pl.loop(0, 32)
    def _(t):
        onehot = jnp.where(rows == kp_ref[t], 1.0, 0.0).astype(jnp.bfloat16)
        psel[t] = jnp.dot(hb_ref[...], onehot, preferred_element_type=jnp.float32).astype(jnp.bfloat16)
        v = urow & kq_ref[t]
        v = v ^ (v >> 4)
        v = v ^ (v >> 2)
        v = v ^ (v >> 1)
        sq[t] = jnp.where((v & 1) == 1, -1.0, 1.0)
    lane = lax.broadcasted_iota(jnp.int32, (8,128), 1)
    sub = lax.broadcasted_iota(jnp.int32, (8,128), 0)
    base = sub*8 + lane//16
    bit_lo = jnp.left_shift(1, lane % 16)
    bit_hi = jnp.left_shift(1, lane % 16 + 16)

    @pl.loop(0, NBLK)
    def _(b):
        slot = b % NS
        for c in copies(b, slot): c.wait()
        @pl.loop(0, UPB//2)
        def _(pair):
            outs = []
            for uu in range(2):
                u = pair*2 + uu
                for j in range(16):
                    wlo = words[slot, j, pl.ds(u, 1), :]
                    whi = words[slot, j+16, pl.ds(u, 1), :]
                    wp = jnp.broadcast_to(wlo | (whi << 16), (8,128))
                    for gam in range(2):
                        y = jnp.take_along_axis(wp, base + gam*64, axis=1)
                        parts = []
                        for hh, bit in ((j, bit_lo), (j+16, bit_hi)):
                            x = raw[slot, hh, :, pl.ds(pl.multiple_of(u*2048 + gam*1024, 1024), 1024)]
                            x = x.astype(jnp.float32).reshape(8,128)
                            parts.append(jnp.where((y & bit) != 0, x, -x))
                        xs[uu, 16*j:16*j+16, gam*128:gam*128+128] = jnp.concatenate(parts, axis=0).astype(jnp.bfloat16)
            for uu in range(2):
                outs.append(jnp.dot(hm_ref[...], xs[uu], preferred_element_type=jnp.float32))
            r0 = pl.multiple_of(b*(UPB*8) + pair*16, 16)
            for t in range(32):
                ts[t, pl.ds(r0, 16), :] = jnp.concatenate([outs[0][8*t:8*t+8], outs[1][8*t:8*t+8]], axis=0).astype(jnp.bfloat16)
        @pl.when(b + NS < NBLK)
        def _():
            for c in copies(b + NS, slot): c.start()

    sub256 = lax.broadcasted_iota(jnp.int32, (8,256), 0)
    @pl.loop(0, 32)
    def _(t):
        u = jnp.dot(ts[t], psel[t], preferred_element_type=jnp.float32)
        total = jnp.zeros((8,256), jnp.float32)
        accs = [jnp.zeros((8,256), jnp.float32) for _ in range(4)]
        for m in range(32):
            s = jnp.broadcast_to(sq[t, m:m+1, :], (8,256))
            for h2 in range(4):
                accs[h2] = accs[h2] + u[h2*256+m*8:h2*256+m*8+8] * s
        for h2 in range(4):
            total = total + accs[h2] * h4_ref[h2:h2+1, :]
        total = jnp.where(sub256 == ks_ref[t], total, 0.0)
        out_ref[pl.ds(t,1), :] = jnp.sum(total, axis=0, keepdims=True)

def sketch_partial(gradients, sign_words, sub_index):
    g = gradients.reshape(32, 4, 1, 65536)
    w = sign_words.reshape(32, 4, 32, 128)
    c = sub_index.reshape(8, 32, 32).transpose(1,0,2).reshape(32,1,256) & 65535
    kp = ((c >> 10) & 1)*128 + (c & 127)
    kq = c >> 11
    ks = (c >> 7) & 7
    col = np.arange(256)
    hh2 = (col >> 3) & 3
    h4 = jnp.asarray(hada(4)[:, hh2], jnp.float32)
    hm = jnp.asarray(k1_matrix(), jnp.bfloat16)
    hb = jnp.asarray(hada(256), jnp.bfloat16)
    anyspec = pl.BlockSpec(memory_space=pl.ANY)
    vm = pl.BlockSpec(memory_space=pltpu.VMEM)
    return pl.pallas_call(
        kernel,
        out_shape=jax.ShapeDtypeStruct((32,256), jnp.float32),
        in_specs=[anyspec, anyspec, vm, vm, vm, vm, vm, vm, vm],
        out_specs=vm,
        scratch_shapes=[
            pltpu.VMEM((NS, 32, 1, FB), jnp.bfloat16),
            pltpu.VMEM((NS, 32, 8, 128), jnp.int32),
            pltpu.VMEM((32, 256, 256), jnp.bfloat16),
            pltpu.VMEM((32, 32, 256), jnp.float32),
            pltpu.VMEM((2, 256, 256), jnp.bfloat16),
            pltpu.VMEM((32, 1024, 256), jnp.bfloat16),
            pltpu.SemaphoreType.DMA((2, NS)),
        ],
        compiler_params=pltpu.CompilerParams(vmem_limit_bytes=60*1024*1024),
    )(g, w, c, kp, kq, ks, h4, hm, hb)

def on_device(gradients, sign_words, sub_index, test_sketch):
    feat = lax.axis_index("feat")
    part = sketch_partial(gradients, sign_words, sub_index)
    g3 = np.arange(256) >> 5
    sgn = jnp.asarray(hada(8)[:, g3], jnp.float32)[feat]
    part = (part * sgn[None, :]).reshape(32, 8, 32).transpose(1,0,2).reshape(1, 8192)
    sketch = lax.psum(part, "feat") * (float(67108864) ** -0.5)
    sk = sketch.astype(jnp.bfloat16)
    allsk = lax.all_gather(sk, "ex", axis=0, tiled=True)
    sc = jnp.einsum("ek,tk->et", allsk, test_sketch, preferred_element_type=jnp.float32)
    sc = sc * (8192.0 ** -0.5)
    out = lax.all_to_all(sc.reshape(16,1,64), "ex", split_axis=0, concat_axis=1, tiled=True)
    return out.reshape(1, 1024)

def solution(mesh):
    return jax.shard_map(on_device, mesh=mesh,
        in_specs=(P("ex", "feat"), P("feat"), P(), P("ex", None)),
        out_specs=P("ex", None), check_vma=False)
```

```python
import jax, jax.numpy as jnp, numpy as np
from jax import lax
from jax.experimental import pallas as pl
from jax.experimental.pallas import tpu as pltpu
from jax.sharding import PartitionSpec as P

def hada(n):
    h=np.ones((1,1))
    while h.shape[0]<n: h=np.block([[h,h],[h,-h]])
    return h

def k1_matrix():
    h32, h8 = hada(32), hada(8)
    rows = np.zeros((256,256))
    for j in range(16):
        for t in range(16):
            h5 = j + 16*(t//8); s = t%8
            rows[:, 16*j+t] = np.kron(h32[:,h5], h8[:,s])
    return rows

FB = 16384
NBLK = 16
NS = 6
UPB = FB//2048

def kernel(g_ref, w_ref, km_ref, kp_ref, kq_ref, ks_ref, h4_ref, hm_ref, hb_ref, out_ref,
           raw, words, psel, sq, xs, ts, sem):
    def copies(b, slot):
        h2 = b // 4
        mb = b % 4
        return (pltpu.make_async_copy(g_ref.at[:, h2, :, pl.ds(mb*FB, FB)], raw.at[slot], sem.at[0, slot]),
                pltpu.make_async_copy(w_ref.at[:, h2, pl.ds(mb*8, 8), :], words.at[slot], sem.at[1, slot]))
    for b in range(NS):
        for c in copies(b, b): c.start()
    rows = lax.broadcasted_iota(jnp.int32, (256,256), 0)
    urow = lax.broadcasted_iota(jnp.int32, (32,256), 0)
    @pl.loop(0, 32)
    def _(t):
        onehot = jnp.where(rows == kp_ref[t], 1.0, 0.0).astype(jnp.bfloat16)
        psel[t] = jnp.dot(hb_ref[...], onehot, preferred_element_type=jnp.float32).astype(jnp.bfloat16)
        v = urow & kq_ref[t]
        v = v ^ (v >> 4)
        v = v ^ (v >> 2)
        v = v ^ (v >> 1)
        sq[t] = jnp.where((v & 1) == 1, -1.0, 1.0)
    lane = lax.broadcasted_iota(jnp.int32, (8,128), 1)
    sub = lax.broadcasted_iota(jnp.int32, (8,128), 0)
    base = sub*8 + lane//16
    bit_lo = jnp.left_shift(1, lane % 16)
    bit_hi = jnp.left_shift(1, lane % 16 + 16)

    @pl.loop(0, NBLK)
    def _(b):
        slot = b % NS
        for c in copies(b, slot): c.wait()
        @pl.loop(0, UPB//2)
        def _(pair):
            outs = []
            for uu in range(2):
                u = pair*2 + uu
                for j in range(16):
                    wlo = words[slot, j, pl.ds(u, 1), :]
                    whi = words[slot, j+16, pl.ds(u, 1), :]
                    wp = jnp.broadcast_to(wlo | (whi << 16), (8,128))
                    for gam in range(2):
                        y = jnp.take_along_axis(wp, base + gam*64, axis=1)
                        parts = []
                        for hh, bit in ((j, bit_lo), (j+16, bit_hi)):
                            x = raw[slot, hh, :, pl.ds(pl.multiple_of(u*2048 + gam*1024, 1024), 1024)]
                            x = x.astype(jnp.float32).reshape(8,128)
                            parts.append(jnp.where((y & bit) != 0, x, -x))
                        xs[uu, 16*j:16*j+16, gam*128:gam*128+128] = jnp.concatenate(parts, axis=0).astype(jnp.bfloat16)
            for uu in range(2):
                outs.append(jnp.dot(hm_ref[...], xs[uu], preferred_element_type=jnp.float32))
            r0 = pl.multiple_of(b*(UPB*8) + pair*16, 16)
            for t in range(32):
                ts[t, pl.ds(r0, 16), :] = jnp.concatenate([outs[0][8*t:8*t+8], outs[1][8*t:8*t+8]], axis=0).astype(jnp.bfloat16)
        @pl.when(b + NS < NBLK)
        def _():
            for c in copies(b + NS, slot): c.start()

    sub256 = lax.broadcasted_iota(jnp.int32, (8,256), 0)
    spread = (sub % 4)*32 + lane % 32
    @pl.loop(0, 8)
    def _(part):
        chunk = jnp.zeros((8,128), jnp.float32)
        for a in range(4):
            t = part*4 + a
            u = jnp.dot(ts[t], psel[t], preferred_element_type=jnp.float32)
            accs = [jnp.zeros((8,256), jnp.float32) for _ in range(4)]
            for m in range(32):
                s = jnp.broadcast_to(sq[t, m:m+1, :], (8,256))
                for h2 in range(4):
                    accs[h2] = accs[h2] + u[h2*256+m*8:h2*256+m*8+8] * s
            total = jnp.zeros((8,256), jnp.float32)
            for h2 in range(4):
                total = total + accs[h2] * h4_ref[h2:h2+1, :]
            total = jnp.where(sub256 == ks_ref[t], total, 0.0)
            row = jnp.broadcast_to(jnp.sum(total, axis=0, keepdims=True), (8,256))
            row = jnp.where(sub < 4, row[:, :128], row[:, 128:])
            row = jnp.take_along_axis(row, spread, axis=1)
            chunk = jnp.where(lane // 32 == a, row, chunk)
        for g in range(8):
            out_ref[g, pl.ds(part, 1), :] = chunk[g:g+1]

def sketch_partial(gradients, sign_words, sub_index):
    g = gradients.reshape(32, 4, 1, 65536)
    w = sign_words.reshape(32, 4, 32, 128)
    c = sub_index.reshape(8, 32, 32).transpose(1,0,2).reshape(32,1,256) & 65535
    kp = ((c >> 10) & 1)*128 + (c & 127)
    kq = c >> 11
    ks = (c >> 7) & 7
    col = np.arange(256)
    hh2 = (col >> 3) & 3
    h4 = jnp.asarray(hada(4)[:, hh2], jnp.float32)
    hm = jnp.asarray(k1_matrix(), jnp.bfloat16)
    hb = jnp.asarray(hada(256), jnp.bfloat16)
    anyspec = pl.BlockSpec(memory_space=pl.ANY)
    vm = pl.BlockSpec(memory_space=pltpu.VMEM)
    return pl.pallas_call(
        kernel,
        out_shape=jax.ShapeDtypeStruct((8,8,128), jnp.float32),
        in_specs=[anyspec, anyspec, vm, vm, vm, vm, vm, vm, vm],
        out_specs=vm,
        scratch_shapes=[
            pltpu.VMEM((NS, 32, 1, FB), jnp.bfloat16),
            pltpu.VMEM((NS, 32, 8, 128), jnp.int32),
            pltpu.VMEM((32, 256, 256), jnp.bfloat16),
            pltpu.VMEM((32, 32, 256), jnp.float32),
            pltpu.VMEM((2, 256, 256), jnp.bfloat16),
            pltpu.VMEM((32, 1024, 256), jnp.bfloat16),
            pltpu.SemaphoreType.DMA((2, NS)),
        ],
        compiler_params=pltpu.CompilerParams(vmem_limit_bytes=60*1024*1024),
        cost_estimate=pl.CostEstimate(flops=17_000_000_000, bytes_accessed=36*1024*1024, transcendentals=0),
    )(g, w, c, kp, kq, ks, h4, hm, hb)

FEATS = 8
MESH = pl.DeviceIdType.MESH

def tail_kernel(part_ref, tests_ref, out_ref, tests, recv1, recv2, mine, send1, got1, send2, got2, tsem):
    me = lax.axis_index("feat")
    tcopy = pltpu.make_async_copy(tests_ref, tests, tsem)
    tcopy.start()
    barrier = pltpu.get_barrier_semaphore()
    peers = [lax.rem(me + d, FEATS) for d in range(1, FEATS)]
    for p in peers:
        pl.semaphore_signal(barrier, inc=1, device_id={"feat": p}, device_id_type=MESH)
    pl.semaphore_wait(barrier, FEATS - 1)
    def first(src, slot, p, d):
        return pltpu.make_async_remote_copy(src_ref=part_ref.at[src], dst_ref=recv1.at[slot], send_sem=send1.at[d],
            recv_sem=got1.at[slot], device_id={"feat": p}, device_id_type=MESH)
    for d, p in enumerate(peers):
        first(p, me, p, d).start()
    recv1[me] = part_ref[me]
    for d, p in enumerate(peers):
        first(p, p, p, d).wait_recv()
    sk = recv1[0]
    for f in range(1, FEATS):
        common = me & f
        parity = (common ^ (common >> 1) ^ (common >> 2)) & 1
        sk = sk + recv1[f] * (1 - 2*parity).astype(jnp.float32)
    sk = sk * (float(67108864) ** -0.5)
    row = jnp.concatenate([sk[g:g+1] for g in range(8)], axis=1)
    lhs = jnp.broadcast_to(row, (16, 1024)).astype(jnp.bfloat16)
    tcopy.wait()
    res = lax.dot_general(lhs, tests[...], (((1,), (1,)), ((), ())), preferred_element_type=jnp.float32)
    mine[...] = res[0:1]
    def second(slot, p, d):
        return pltpu.make_async_remote_copy(src_ref=mine, dst_ref=recv2.at[slot], send_sem=send2.at[d],
            recv_sem=got2.at[slot], device_id={"feat": p}, device_id_type=MESH)
    for d, p in enumerate(peers):
        second(me, p, d).start()
    recv2[me] = res[0:1]
    for d, p in enumerate(peers):
        second(p, p, d).wait_recv()
    total = recv2[0]
    for f in range(1, FEATS):
        total = total + recv2[f]
    out_ref[...] = total * (8192.0 ** -0.5)
    for d, p in enumerate(peers):
        first(p, me, p, d).wait_send()
        second(me, p, d).wait_send()

def scores_of(part, tests):
    vm = pl.BlockSpec(memory_space=pltpu.VMEM)
    return pl.pallas_call(
        tail_kernel,
        out_shape=jax.ShapeDtypeStruct((1,1024), jnp.float32),
        in_specs=[vm, pl.BlockSpec(memory_space=pl.ANY)],
        out_specs=vm,
        scratch_shapes=[
            pltpu.VMEM((1024, 1024), jnp.bfloat16),
            pltpu.VMEM((FEATS, 8, 128), jnp.float32),
            pltpu.VMEM((FEATS, 1, 1024), jnp.float32),
            pltpu.VMEM((1, 1024), jnp.float32),
            pltpu.SemaphoreType.DMA((FEATS - 1,)),
            pltpu.SemaphoreType.DMA((FEATS,)),
            pltpu.SemaphoreType.DMA((FEATS - 1,)),
            pltpu.SemaphoreType.DMA((FEATS,)),
            pltpu.SemaphoreType.DMA,
        ],
        compiler_params=pltpu.CompilerParams(collective_id=0, has_side_effects=True, vmem_limit_bytes=60*1024*1024),
    )(part, tests)

def on_device(gradients, sign_words, sub_index, test_sketch):
    feat = lax.axis_index("feat")
    cols = lax.dynamic_slice_in_dim(test_sketch, feat*1024, 1024, axis=1)
    tests = lax.all_gather(cols, "ex", axis=0, tiled=True)
    part = sketch_partial(gradients, sign_words, sub_index)
    return scores_of(part, tests)

def solution(mesh):
    return jax.shard_map(on_device, mesh=mesh,
        in_specs=(P("ex", "feat"), P("feat"), P(), P("ex", None)),
        out_specs=P("ex", None), check_vma=False)
```

```python
import jax, jax.numpy as jnp, numpy as np
from jax import lax
from jax.experimental import pallas as pl
from jax.experimental.pallas import tpu as pltpu
from jax.sharding import PartitionSpec as P

def hada(n):
    h=np.ones((1,1))
    while h.shape[0]<n: h=np.block([[h,h],[h,-h]])
    return h

def k1_matrix():
    h32, h8 = hada(32), hada(8)
    rows = np.zeros((256,256))
    for j in range(16):
        for t in range(16):
            h5 = j + 16*(t//8); s = t%8
            rows[:, 16*j+t] = np.kron(h32[:,h5], h8[:,s])
    return rows

FB = 8192
NBLK = 32
NS = 12
UNITS = 4
TUNROLL = 4

def kernel(g_ref, w_ref, kp_ref, kq_ref, ks_ref, h4_ref, hm_ref, hb_ref, out_ref,
           raw, words, psel, sq, xs0, xs1, ts, sem, wsem):
    def gcopy(b):
        return pltpu.make_async_copy(g_ref.at[:, b // 8, :, pl.ds(pl.multiple_of((b % 8)*FB, FB), FB)], raw.at[b % NS], sem.at[b % NS])
    def wcopy(h2):
        return pltpu.make_async_copy(w_ref.at[:, h2], words.at[h2], wsem.at[h2])
    wcopy(0).start()
    for b in range(NS):
        gcopy(b).start()
    for h2 in range(1, 4):
        wcopy(h2).start()
    rows = lax.broadcasted_iota(jnp.int32, (256,256), 0)
    urow = lax.broadcasted_iota(jnp.int32, (32,256), 0)
    @pl.loop(0, 32//TUNROLL)
    def _(tt):
        for dt in range(TUNROLL):
            t = tt*TUNROLL + dt
            onehot = jnp.where(rows == kp_ref[t], 1.0, 0.0).astype(jnp.bfloat16)
            psel[t] = jnp.dot(hb_ref[...], onehot, preferred_element_type=jnp.float32).astype(jnp.bfloat16)
            v = urow & kq_ref[t]
            v = v ^ (v >> 4)
            v = v ^ (v >> 2)
            v = v ^ (v >> 1)
            sq[t] = jnp.where((v & 1) == 1, -1.0, 1.0)
    lane = lax.broadcasted_iota(jnp.int32, (8,128), 1)
    sub = lax.broadcasted_iota(jnp.int32, (8,128), 0)
    base = sub*8 + lane//16
    bit_lo = jnp.left_shift(1, lane % 16)
    bit_hi = jnp.left_shift(1, lane % 16 + 16)

    def prep(b, xs):
        slot = b % NS
        h2 = b // 8
        r0 = (b % 8)*UNITS
        for u in range(UNITS):
            for j in range(16):
                wlo = words[h2, j, pl.ds(r0 + u, 1), :]
                whi = words[h2, j+16, pl.ds(r0 + u, 1), :]
                wp = jnp.broadcast_to(wlo | (whi << 16), (8,128))
                for gam in range(2):
                    y = jnp.take_along_axis(wp, base + gam*64, axis=1)
                    parts = []
                    for hh, bit in ((j, bit_lo), (j+16, bit_hi)):
                        x = raw[slot, hh, :, u*2048 + gam*1024:u*2048 + gam*1024+1024]
                        x = x.astype(jnp.float32).reshape(8,128)
                        parts.append(jnp.where((y & bit) != 0, x, -x))
                    xs[16*j:16*j+16, u*256+gam*128:u*256+gam*128+128] = jnp.concatenate(parts, axis=0).astype(jnp.bfloat16)

    def mix(b, xs):
        for pair in range(UNITS//2):
            outs = [jnp.dot(hm_ref[...], xs[:, (2*pair+uu)*256:(2*pair+uu)*256+256], preferred_element_type=jnp.float32) for uu in range(2)]
            r0 = pl.multiple_of(b*(UNITS*8) + pair*16, 16)
            for t in range(32):
                ts[t, pl.ds(r0, 16), :] = jnp.concatenate([outs[0][8*t:8*t+8], outs[1][8*t:8*t+8]], axis=0).astype(jnp.bfloat16)

    def arrive(b):
        @pl.when(b < NBLK)
        def _():
            gcopy(b).wait()
        @pl.when((b < NBLK) & (b % 8 == 0))
        def _():
            wcopy(b // 8).wait()
    def refill(b):
        @pl.when(b < NBLK)
        def _():
            gcopy(b).start()

    arrive(0)
    prep(0, xs0)
    refill(NS)
    @pl.loop(0, NBLK//2)
    def _(i):
        b = 2*i
        arrive(b + 1)
        prep(b + 1, xs1)
        mix(b, xs0)
        refill(b + 1 + NS)
        arrive(b + 2)
        prep(jnp.minimum(b + 2, NBLK - 1), xs0)
        mix(b + 1, xs1)
        refill(b + 2 + NS)

    sub256 = lax.broadcasted_iota(jnp.int32, (8,256), 0)
    spread = (sub % 4)*32 + lane % 32
    @pl.loop(0, 8)
    def _(part):
        chunk = jnp.zeros((8,128), jnp.float32)
        for a in range(4):
            t = part*4 + a
            u = jnp.dot(ts[t], psel[t], preferred_element_type=jnp.float32)
            accs = [jnp.zeros((8,256), jnp.float32) for _ in range(4)]
            for m in range(32):
                s = jnp.broadcast_to(sq[t, m:m+1, :], (8,256))
                for h2 in range(4):
                    accs[h2] = accs[h2] + u[h2*256+m*8:h2*256+m*8+8] * s
            total = jnp.zeros((8,256), jnp.float32)
            for h2 in range(4):
                total = total + accs[h2] * h4_ref[h2:h2+1, :]
            total = jnp.where(sub256 == ks_ref[t], total, 0.0)
            row = jnp.broadcast_to(jnp.sum(total, axis=0, keepdims=True), (8,256))
            row = jnp.where(sub < 4, row[:, :128], row[:, 128:])
            row = jnp.take_along_axis(row, spread, axis=1)
            chunk = jnp.where(lane // 32 == a, row, chunk)
        for g in range(8):
            out_ref[g, pl.ds(part, 1), :] = chunk[g:g+1]

def sketch_partial(gradients, sign_words, sub_index):
    g = gradients.reshape(32, 4, 1, 65536)
    w = sign_words.reshape(32, 4, 32, 128)
    c = sub_index.reshape(8, 32, 32).transpose(1,0,2).reshape(32,1,256) & 65535
    kp = ((c >> 10) & 1)*128 + (c & 127)
    kq = c >> 11
    ks = (c >> 7) & 7
    col = np.arange(256)
    hh2 = (col >> 3) & 3
    h4 = jnp.asarray(hada(4)[:, hh2], jnp.float32)
    hm = jnp.asarray(k1_matrix(), jnp.bfloat16)
    hb = jnp.asarray(hada(256), jnp.bfloat16)
    anyspec = pl.BlockSpec(memory_space=pl.ANY)
    vm = pl.BlockSpec(memory_space=pltpu.VMEM)
    return pl.pallas_call(
        kernel,
        out_shape=jax.ShapeDtypeStruct((8,8,128), jnp.float32),
        in_specs=[anyspec, anyspec, vm, vm, vm, vm, vm, vm],
        out_specs=vm,
        scratch_shapes=[
            pltpu.VMEM((NS, 32, 1, FB), jnp.bfloat16),
            pltpu.VMEM((4, 32, 32, 128), jnp.int32),
            pltpu.VMEM((32, 256, 256), jnp.bfloat16),
            pltpu.VMEM((32, 32, 256), jnp.float32),
            pltpu.VMEM((256, UNITS*256), jnp.bfloat16),
            pltpu.VMEM((256, UNITS*256), jnp.bfloat16),
            pltpu.VMEM((32, 1024, 256), jnp.bfloat16),
            pltpu.SemaphoreType.DMA((NS,)),
            pltpu.SemaphoreType.DMA((4,)),
        ],
        compiler_params=pltpu.CompilerParams(vmem_limit_bytes=60*1024*1024),
        cost_estimate=pl.CostEstimate(flops=17_000_000_000, bytes_accessed=36*1024*1024, transcendentals=0),
    )(g, w, kp, kq, ks, h4, hm, hb)

FEATS, EXS = 8, 16
MESH = pl.DeviceIdType.MESH

def tail_kernel(part_ref, tests_ref, out_ref, tests, recv1, recv2, recv3, recv4, mine1, mine2,
                send1, got1, send2, got2, send3, got3, send4, got4, tsem):
    feat = lax.axis_index("feat")
    ex = lax.axis_index("ex")
    tcopy = pltpu.make_async_copy(tests_ref.at[:, pl.ds(pl.multiple_of(feat*1024, 1024), 1024)], tests, tsem)
    tcopy.start()
    barrier = pltpu.get_barrier_semaphore()
    fpeers = [lax.rem(feat + d, FEATS) for d in range(1, FEATS)]
    epeers = [lax.rem(ex + d, EXS) for d in range(1, EXS)]
    for p in fpeers:
        pl.semaphore_signal(barrier, inc=1, device_id={"feat": p}, device_id_type=MESH)
    for p in epeers:
        pl.semaphore_signal(barrier, inc=1, device_id={"ex": p}, device_id_type=MESH)
    pl.semaphore_wait(barrier, FEATS + EXS - 2)

    def exchange(peers, axis, src_of, dst, send, got):
        me = feat if axis == "feat" else ex
        def copy(slot, p, d):
            return pltpu.make_async_remote_copy(src_ref=src_of(p), dst_ref=dst.at[slot], send_sem=send.at[d],
                recv_sem=got.at[slot], device_id={axis: p}, device_id_type=MESH)
        sent = [copy(me, p, d) for d, p in enumerate(peers)]
        for c in sent:
            c.start()
        return sent, [copy(p, p, d) for d, p in enumerate(peers)]

    waits = []
    sent, come = exchange(fpeers, "feat", lambda p: part_ref.at[p], recv1, send1, got1)
    waits += sent
    recv1[feat] = part_ref[feat]
    for c in come: c.wait_recv()
    sk = jnp.zeros((8,128), jnp.float32)
    for f in range(FEATS):
        common = feat & f
        parity = (common ^ (common >> 1) ^ (common >> 2)) & 1
        sk = sk + recv1[f] * (1 - 2*parity).astype(jnp.float32)
    sk = sk * (float(67108864) ** -0.5)
    sk = sk.astype(jnp.bfloat16).astype(jnp.float32)
    mine1[...] = sk
    sent, come = exchange(epeers, "ex", lambda p: mine1, recv2, send2, got2)
    waits += sent
    recv2[ex] = sk
    tcopy.wait()
    for c in come: c.wait_recv()
    res = jnp.zeros((EXS, 64), jnp.float32)
    for g in range(8):
        lhs = recv2[:, g, :].astype(jnp.bfloat16)
        res = res + lax.dot_general(lhs, tests[:, g*128:g*128+128], (((1,), (1,)), ((), ())), preferred_element_type=jnp.float32)
    wide = jnp.concatenate([res, res], axis=1)
    half = lax.broadcasted_iota(jnp.int32, (EXS, 128), 1) // 64
    wide = jnp.where(half == lax.rem(ex, 2), wide, 0.0)
    for e in range(EXS):
        mine2[e] = wide[e:e+1]
    sent, come = exchange(epeers, "ex", lambda p: mine2.at[p], recv3, send3, got3)
    waits += sent
    recv3[ex] = mine2[ex]
    for c in come: c.wait_recv()
    for j in range(8):
        mine1b = recv3[2*j] + recv3[2*j+1]
        recv4[feat, pl.ds(j, 1), :] = mine1b
    sent, come = exchange(fpeers, "feat", lambda p: recv4.at[feat], recv4, send4, got4)
    waits += sent
    for c in come: c.wait_recv()
    total = recv4[0]
    for f in range(1, FEATS):
        total = total + recv4[f]
    out_ref[...] = total
    for c in waits:
        c.wait_send()

def scores_of(part, tests):
    vm = pl.BlockSpec(memory_space=pltpu.VMEM)
    dma = pltpu.SemaphoreType.DMA
    return pl.pallas_call(
        tail_kernel,
        out_shape=jax.ShapeDtypeStruct((8,128), jnp.float32),
        in_specs=[vm, pl.BlockSpec(memory_space=pl.ANY)],
        out_specs=vm,
        scratch_shapes=[
            pltpu.VMEM((64, 1024), jnp.bfloat16),
            pltpu.VMEM((FEATS, 8, 128), jnp.float32),
            pltpu.VMEM((EXS, 8, 128), jnp.float32),
            pltpu.VMEM((EXS, 1, 128), jnp.float32),
            pltpu.VMEM((FEATS, 8, 128), jnp.float32),
            pltpu.VMEM((8, 128), jnp.float32),
            pltpu.VMEM((EXS, 1, 128), jnp.float32),
            dma((FEATS - 1,)), dma((FEATS,)), dma((EXS - 1,)), dma((EXS,)),
            dma((EXS - 1,)), dma((EXS,)), dma((FEATS - 1,)), dma((FEATS,)), dma,
        ],
        compiler_params=pltpu.CompilerParams(collective_id=0, has_side_effects=True, vmem_limit_bytes=60*1024*1024),
    )(part, tests)

def on_device(gradients, sign_words, sub_index, test_sketch):
    part = sketch_partial(gradients, sign_words, sub_index)
    return (scores_of(part, test_sketch) * (8192.0 ** -0.5)).reshape(1, 1024)

def solution(mesh):
    return jax.shard_map(on_device, mesh=mesh,
        in_specs=(P("ex", "feat"), P("feat"), P(), P("ex", None)),
        out_specs=P("ex", None), check_vma=False)
```

```python
import jax, jax.numpy as jnp, numpy as np
from jax import lax
from jax.experimental import pallas as pl
from jax.experimental.pallas import tpu as pltpu
from jax.sharding import PartitionSpec as P

def hada(n):
    h=np.ones((1,1))
    while h.shape[0]<n: h=np.block([[h,h],[h,-h]])
    return h

def k1_matrix():
    h32, h8 = hada(32), hada(8)
    rows = np.zeros((256,256))
    for j in range(16):
        for t in range(16):
            h5 = j + 16*(t//8); s = t%8
            rows[:, 16*j+t] = np.kron(h32[:,h5], h8[:,s])
    return rows

FB = 8192
NBLK = 32
NS = 12
UNITS = 4
TUNROLL = 4

FEATS, EXS = 8, 16
MESH = pl.DeviceIdType.MESH

def kernel(g_ref, w_ref, kp_ref, kq_ref, ks_ref, h4_ref, hm_ref, hb_ref, t_ref, out_ref,
           raw, words, psel, sq, xs0, xs1, ts, tests, mine1, recv1, mine2, recv2, sem, wsem,
           tsem, send0, got0, send1, got1, send2, got2):
    feat = lax.axis_index("feat")
    ex = lax.axis_index("ex")
    fpeers = [lax.rem(feat + d, FEATS) for d in range(1, FEATS)]
    epeers = [lax.rem(ex + d, EXS) for d in range(1, EXS)]
    barrier = pltpu.get_barrier_semaphore()
    for p in fpeers:
        pl.semaphore_signal(barrier, inc=1, device_id={"feat": p}, device_id_type=MESH)
    for p in epeers:
        pl.semaphore_signal(barrier, inc=1, device_id={"ex": p}, device_id_type=MESH)
    def tcopy(g):
        return pltpu.make_async_copy(t_ref.at[:, pl.ds(pl.multiple_of(g*1024 + feat*128, 128), 128)],
            tests.at[ex, :, g*128:g*128+128], tsem.at[g])
    def remote(src, dst, send, got, axis, p):
        return pltpu.make_async_remote_copy(src_ref=src, dst_ref=dst, send_sem=send, recv_sem=got,
            device_id={axis: p}, device_id_type=MESH)
    def gcopy(b):
        return pltpu.make_async_copy(g_ref.at[:, b // 8, :, pl.ds(pl.multiple_of((b % 8)*FB, FB), FB)], raw.at[b % NS], sem.at[b % NS])
    def wcopy(h2):
        return pltpu.make_async_copy(w_ref.at[:, h2], words.at[h2], wsem.at[h2])
    wcopy(0).start()
    for b in range(NS):
        gcopy(b).start()
    for h2 in range(1, 4):
        wcopy(h2).start()
    for g in range(8):
        tcopy(g).start()
    rows = lax.broadcasted_iota(jnp.int32, (256,256), 0)
    urow = lax.broadcasted_iota(jnp.int32, (32,256), 0)
    @pl.loop(0, 32//TUNROLL)
    def _(tt):
        for dt in range(TUNROLL):
            t = tt*TUNROLL + dt
            onehot = jnp.where(rows == kp_ref[t], 1.0, 0.0).astype(jnp.bfloat16)
            psel[t] = jnp.dot(hb_ref[...], onehot, preferred_element_type=jnp.float32).astype(jnp.bfloat16)
            v = urow & kq_ref[t]
            v = v ^ (v >> 4)
            v = v ^ (v >> 2)
            v = v ^ (v >> 1)
            sq[t] = jnp.where((v & 1) == 1, -1.0, 1.0)
    lane = lax.broadcasted_iota(jnp.int32, (8,128), 1)
    sub = lax.broadcasted_iota(jnp.int32, (8,128), 0)
    base = sub*8 + lane//16
    bit_lo = jnp.left_shift(1, lane % 16)
    bit_hi = jnp.left_shift(1, lane % 16 + 16)

    def prep(b, xs):
        slot = b % NS
        h2 = b // 8
        r0 = (b % 8)*UNITS
        for u in range(UNITS):
            for j in range(16):
                wlo = words[h2, j, pl.ds(r0 + u, 1), :]
                whi = words[h2, j+16, pl.ds(r0 + u, 1), :]
                wp = jnp.broadcast_to(wlo | (whi << 16), (8,128))
                for gam in range(2):
                    y = jnp.take_along_axis(wp, base + gam*64, axis=1)
                    parts = []
                    for hh, bit in ((j, bit_lo), (j+16, bit_hi)):
                        x = raw[slot, hh, :, u*2048 + gam*1024:u*2048 + gam*1024+1024]
                        x = x.astype(jnp.float32).reshape(8,128)
                        parts.append(jnp.where((y & bit) != 0, x, -x))
                    xs[16*j:16*j+16, u*256+gam*128:u*256+gam*128+128] = jnp.concatenate(parts, axis=0).astype(jnp.bfloat16)

    def mix(b, xs):
        for pair in range(UNITS//2):
            outs = [jnp.dot(hm_ref[...], xs[:, (2*pair+uu)*256:(2*pair+uu)*256+256], preferred_element_type=jnp.float32) for uu in range(2)]
            r0 = pl.multiple_of(b*(UNITS*8) + pair*16, 16)
            for t in range(32):
                ts[t, pl.ds(r0, 16), :] = jnp.concatenate([outs[0][8*t:8*t+8], outs[1][8*t:8*t+8]], axis=0).astype(jnp.bfloat16)

    def arrive(b):
        @pl.when(b < NBLK)
        def _():
            gcopy(b).wait()
        @pl.when((b < NBLK) & (b % 8 == 0))
        def _():
            wcopy(b // 8).wait()
    def refill(b):
        @pl.when(b < NBLK)
        def _():
            gcopy(b).start()

    pl.semaphore_wait(barrier, FEATS + EXS - 2)
    for g in range(8):
        tcopy(g).wait()
    for d, p in enumerate(epeers):
        remote(tests.at[ex], tests.at[ex], send0.at[d], got0.at[ex], "ex", p).start()
    arrive(0)
    prep(0, xs0)
    refill(NS)
    @pl.loop(0, NBLK//2)
    def _(i):
        b = 2*i
        arrive(b + 1)
        prep(b + 1, xs1)
        mix(b, xs0)
        refill(b + 1 + NS)
        arrive(b + 2)
        prep(jnp.minimum(b + 2, NBLK - 1), xs0)
        mix(b + 1, xs1)
        refill(b + 2 + NS)

    sub256 = lax.broadcasted_iota(jnp.int32, (8,256), 0)
    spread = (sub % 4)*32 + lane % 32
    @pl.loop(0, 8)
    def _(i):
        part = lax.rem(feat + 1 + i, FEATS)
        chunk = jnp.zeros((8,128), jnp.float32)
        for a in range(4):
            t = part*4 + a
            u = jnp.dot(ts[t], psel[t], preferred_element_type=jnp.float32)
            accs = [jnp.zeros((8,256), jnp.float32) for _ in range(4)]
            for m in range(32):
                s = jnp.broadcast_to(sq[t, m:m+1, :], (8,256))
                for h2 in range(4):
                    accs[h2] = accs[h2] + u[h2*256+m*8:h2*256+m*8+8] * s
            total = jnp.zeros((8,256), jnp.float32)
            for h2 in range(4):
                total = total + accs[h2] * h4_ref[h2:h2+1, :]
            total = jnp.where(sub256 == ks_ref[t], total, 0.0)
            row = jnp.broadcast_to(jnp.sum(total, axis=0, keepdims=True), (8,256))
            row = jnp.where(sub < 4, row[:, :128], row[:, 128:])
            row = jnp.take_along_axis(row, spread, axis=1)
            chunk = jnp.where(lane // 32 == a, row, chunk)
        mine1[part] = chunk
        @pl.when(i < FEATS - 1)
        def _():
            remote(mine1.at[part], recv1.at[feat], send1.at[i], got1.at[feat], "feat", part).start()

    recv1[feat] = mine1[feat]
    for d, p in enumerate(epeers):
        remote(tests.at[p], tests.at[p], send0.at[d], got0.at[p], "ex", p).wait_recv()
    for d, p in enumerate(fpeers):
        remote(mine1.at[p], recv1.at[p], send1.at[d], got1.at[p], "feat", p).wait_recv()
    sk = jnp.zeros((8,128), jnp.float32)
    for f in range(FEATS):
        v = sub & f
        v = (v ^ (v >> 1) ^ (v >> 2)) & 1
        sk = sk + jnp.where(v == 1, -recv1[f], recv1[f])
    sk = sk * (float(67108864) ** -0.5)
    row = jnp.concatenate([sk[g:g+1] for g in range(8)], axis=1)
    lhs = jnp.broadcast_to(row, (16, 1024)).astype(jnp.bfloat16)
    res = lax.dot_general(lhs, tests[...].reshape(1024, 1024), (((1,), (1,)), ((), ())), preferred_element_type=jnp.float32)
    mine2[...] = res[0:1]
    for d, p in enumerate(fpeers):
        remote(mine2, recv2.at[feat], send2.at[d], got2.at[feat], "feat", p).start()
    recv2[feat] = res[0:1]
    for d, p in enumerate(fpeers):
        remote(mine2, recv2.at[p], send2.at[d], got2.at[p], "feat", p).wait_recv()
    total = recv2[0]
    for f in range(1, FEATS):
        total = total + recv2[f]
    out_ref[...] = total
    for d, p in enumerate(epeers):
        remote(tests.at[ex], tests.at[ex], send0.at[d], got0.at[ex], "ex", p).wait_send()
    for d, p in enumerate(fpeers):
        remote(mine1.at[p], recv1.at[feat], send1.at[d], got1.at[feat], "feat", p).wait_send()
        remote(mine2, recv2.at[feat], send2.at[d], got2.at[feat], "feat", p).wait_send()

def scores_of(gradients, sign_words, sub_index, test_sketch):
    g = gradients.reshape(32, 4, 1, 65536)
    w = sign_words.reshape(32, 4, 32, 128)
    c = sub_index.reshape(8, 32, 32).transpose(1,0,2).reshape(32,1,256) & 65535
    kp = ((c >> 10) & 1)*128 + (c & 127)
    kq = c >> 11
    ks = (c >> 7) & 7
    col = np.arange(256)
    hh2 = (col >> 3) & 3
    h4 = jnp.asarray(hada(4)[:, hh2], jnp.float32)
    hm = jnp.asarray(k1_matrix(), jnp.bfloat16)
    hb = jnp.asarray(hada(256), jnp.bfloat16)
    anyspec = pl.BlockSpec(memory_space=pl.ANY)
    vm = pl.BlockSpec(memory_space=pltpu.VMEM)
    dma = pltpu.SemaphoreType.DMA
    return pl.pallas_call(
        kernel,
        out_shape=jax.ShapeDtypeStruct((1,1024), jnp.float32),
        in_specs=[anyspec, anyspec, vm, vm, vm, vm, vm, vm, anyspec],
        out_specs=vm,
        scratch_shapes=[
            pltpu.VMEM((NS, 32, 1, FB), jnp.bfloat16),
            pltpu.VMEM((4, 32, 32, 128), jnp.int32),
            pltpu.VMEM((32, 256, 256), jnp.bfloat16),
            pltpu.VMEM((32, 32, 256), jnp.float32),
            pltpu.VMEM((256, UNITS*256), jnp.bfloat16),
            pltpu.VMEM((256, UNITS*256), jnp.bfloat16),
            pltpu.VMEM((32, 1024, 256), jnp.bfloat16),
            pltpu.VMEM((EXS, 64, 1024), jnp.bfloat16),
            pltpu.VMEM((FEATS, 8, 128), jnp.float32),
            pltpu.VMEM((FEATS, 8, 128), jnp.float32),
            pltpu.VMEM((1, 1024), jnp.float32),
            pltpu.VMEM((FEATS, 1, 1024), jnp.float32),
            dma((NS,)), dma((4,)), dma((8,)), dma((EXS - 1,)), dma((EXS,)),
            dma((FEATS - 1,)), dma((FEATS,)), dma((FEATS - 1,)), dma((FEATS,)),
        ],
        compiler_params=pltpu.CompilerParams(collective_id=0, has_side_effects=True, vmem_limit_bytes=60*1024*1024),
        cost_estimate=pl.CostEstimate(flops=17_000_000_000, bytes_accessed=36*1024*1024, transcendentals=0),
    )(g, w, kp, kq, ks, h4, hm, hb, test_sketch)

def on_device(gradients, sign_words, sub_index, test_sketch):
    return scores_of(gradients, sign_words, sub_index, test_sketch) * (8192.0 ** -0.5)

def solution(mesh):
    return jax.shard_map(on_device, mesh=mesh,
        in_specs=(P("ex", "feat"), P("feat"), P(), P("ex", None)),
        out_specs=P("ex", None), check_vma=False)
```

```python
import jax, jax.numpy as jnp, numpy as np
from jax import lax
from jax.experimental import pallas as pl
from jax.experimental.pallas import tpu as pltpu
from jax.sharding import PartitionSpec as P

def hada(n):
    h=np.ones((1,1))
    while h.shape[0]<n: h=np.block([[h,h],[h,-h]])
    return h

def k1_matrix():
    h32, h8 = hada(32), hada(8)
    rows = np.zeros((256,256))
    for j in range(16):
        for t in range(16):
            h5 = j + 16*(t//8); s = t%8
            rows[:, 16*j+t] = np.kron(h32[:,h5], h8[:,s])
    return rows

FB = 8192
NBLK = 32
NS = 12
UNITS = 4
TUNROLL = 4

FEATS, EXS, XS = 8, 16, 4
MESH = pl.DeviceIdType.MESH

def kernel(g_ref, w_ref, kp_ref, kq_ref, ks_ref, h4_ref, hm_ref, hb_ref, t_ref, out_ref,
           raw, words, psel, sq, xs0, xs1, tsa, tsb, acc, tstage, tests, mine1, recv1, mine2, recv2, sem, wsem,
           tsem, send0, got0, send1, got1, send2, got2):
    feat = lax.axis_index("feat")
    ex = lax.axis_index("ex")
    xpos = lax.rem(ex, XS)
    zpos = ex // XS
    group = [(df, dx, lax.rem(feat + df, FEATS), lax.rem(xpos + dx, XS)) for df in range(FEATS) for dx in range(XS) if df or dx]
    epeers = [lax.rem(ex + d, EXS) for d in range(1, EXS)]
    far = [lax.rem(zpos + dz, EXS // XS)*XS + x for dz in range(1, EXS // XS) for x in range(XS)]
    me = feat*XS + xpos
    barrier = pltpu.get_barrier_semaphore()
    for _, _, f, x in group:
        pl.semaphore_signal(barrier, inc=1, device_id=(f, zpos*XS + x), device_id_type=MESH)
    for e in far:
        pl.semaphore_signal(barrier, inc=1, device_id=(feat, e), device_id_type=MESH)
    def tcopy(x, r):
        return pltpu.make_async_copy(t_ref.at[:, pl.ds(pl.multiple_of((2*x + r)*1024 + feat*128, 128), 128)],
            tstage.at[x, :, r*128:r*128+128], tsem.at[2*x + r])
    def remote(src, dst, send, got, f, e):
        return pltpu.make_async_remote_copy(src_ref=src, dst_ref=dst, send_sem=send, recv_sem=got,
            device_id=(f, e), device_id_type=MESH)
    def to_tests(d, e, slot):
        return remote(tstage.at[lax.rem(e, XS)], tests.at[slot], send0.at[d], got0.at[slot], feat, e)
    def to_share(i, dx, f, x, slot):
        return remote(mine1.at[f, x], recv1.at[slot], send1.at[i*XS + dx], got1.at[slot], f, zpos*XS + x)
    def to_score(df, dx, f, x, slot):
        return remote(mine2.at[x], recv2.at[slot], send2.at[df*XS + dx], got2.at[slot], f, zpos*XS + x)
    def gcopy(b):
        return pltpu.make_async_copy(g_ref.at[:, b // 8, :, pl.ds(pl.multiple_of((b % 8)*FB, FB), FB)], raw.at[b % NS], sem.at[b % NS])
    def wcopy(h2):
        return pltpu.make_async_copy(w_ref.at[:, h2], words.at[h2], wsem.at[h2])
    wcopy(0).start()
    for b in range(NS):
        gcopy(b).start()
    for h2 in range(1, 4):
        wcopy(h2).start()
    for x in range(XS):
        for r in range(2):
            tcopy(x, r).start()
    rows = lax.broadcasted_iota(jnp.int32, (256,256), 0)
    urow = lax.broadcasted_iota(jnp.int32, (32,256), 0)
    @pl.loop(0, 32//TUNROLL)
    def _(tt):
        for dt in range(TUNROLL):
            t = tt*TUNROLL + dt
            onehot = jnp.where(rows == kp_ref[t], 1.0, 0.0).astype(jnp.bfloat16)
            psel[t] = jnp.dot(hb_ref[...], onehot, preferred_element_type=jnp.float32).astype(jnp.bfloat16)
            v = urow & kq_ref[t]
            v = v ^ (v >> 4)
            v = v ^ (v >> 2)
            v = v ^ (v >> 1)
            sq[t] = jnp.where((v & 1) == 1, -1.0, 1.0)
    lane = lax.broadcasted_iota(jnp.int32, (8,128), 1)
    sub = lax.broadcasted_iota(jnp.int32, (8,128), 0)
    base = sub*8 + lane//16
    bit_lo = jnp.left_shift(1, lane % 16)
    bit_hi = jnp.left_shift(1, lane % 16 + 16)

    def prep(b, xs):
        slot = b % NS
        h2 = b // 8
        r0 = (b % 8)*UNITS
        for u in range(UNITS):
            for j in range(16):
                wlo = words[h2, j, pl.ds(r0 + u, 1), :]
                whi = words[h2, j+16, pl.ds(r0 + u, 1), :]
                wp = jnp.broadcast_to(wlo | (whi << 16), (8,128))
                for gam in range(2):
                    y = jnp.take_along_axis(wp, base + gam*64, axis=1)
                    parts = []
                    for hh, bit in ((j, bit_lo), (j+16, bit_hi)):
                        x = raw[slot, hh, :, u*2048 + gam*1024:u*2048 + gam*1024+1024]
                        x = x.astype(jnp.float32).reshape(8,128)
                        parts.append(jnp.where((y & bit) != 0, x, -x))
                    xs[2*u + gam, 16*j:16*j+16, :] = jnp.concatenate(parts, axis=0).astype(jnp.bfloat16)

    def mix(b, xs, ts):
        for pair in range(UNITS//2):
            outs = [jnp.dot(hm_ref[...], jnp.concatenate([xs[4*pair + 2*uu], xs[4*pair + 2*uu + 1]], axis=1), preferred_element_type=jnp.float32) for uu in range(2)]
            r0 = pl.multiple_of((b % 8)*(UNITS*8) + pair*16, 16)
            for t in range(32):
                for half in range(2):
                    c = half*128
                    ts[t, half, pl.ds(r0, 16), :] = jnp.concatenate([outs[0][8*t:8*t+8, c:c+128], outs[1][8*t:8*t+8, c:c+128]], axis=0).astype(jnp.bfloat16)

    def pick(h2, t, ts):
        u = jnp.dot(jnp.concatenate([ts[t, 0], ts[t, 1]], axis=1), psel[t], preferred_element_type=jnp.float32)
        tot = jnp.zeros((8,256), jnp.float32)
        for m in range(32):
            tot = tot + u[8*m:8*m+8] * jnp.broadcast_to(sq[t, m:m+1, :], (8,256))
        return tot * h4_ref[h2:h2+1, :]

    def arrive(b):
        @pl.when(b < NBLK)
        def _():
            gcopy(b).wait()
        @pl.when((b < NBLK) & (b % 8 == 0))
        def _():
            wcopy(b // 8).wait()
    def refill(b):
        @pl.when(b < NBLK)
        def _():
            gcopy(b).start()

    arrive(0)
    prep(0, xs0)
    refill(NS)
    for h2 in range(4):
        new, old = (tsa, tsb) if h2 % 2 == 0 else (tsb, tsa)
        @pl.loop(0, 4)
        def _(i):
            b = 8*h2 + 2*i
            if h2 == 0:
                @pl.when(i == 1)
                def _():
                    pl.semaphore_wait(barrier, len(group) + len(far))
                    for x in range(XS):
                        for r in range(2):
                            tcopy(x, r).wait()
                    for d, e in enumerate(epeers):
                        to_tests(d, e, ex).start()
            arrive(b + 1)
            arrive(b + 2)
            for k, (xa, xb) in enumerate(((xs1, xs0), (xs0, xs1))):
                prep(jnp.minimum(b + k + 1, NBLK - 1), xa)
                mix(b + k, xb, new)
                if h2 > 0:
                    for dt in range(4):
                        t = 8*i + 4*k + dt
                        val = pick(h2 - 1, t, old)
                        acc[t] = val if h2 == 1 else acc[t] + val
            refill(b + 1 + NS)
            refill(b + 2 + NS)

    sub256 = lax.broadcasted_iota(jnp.int32, (8,256), 0)
    spread = (sub % 4)*32 + lane % 32
    @pl.loop(0, 8)
    def _(i):
        part = lax.rem(feat + 1 + i, FEATS)
        chunk = jnp.zeros((8,128), jnp.float32)
        for a in range(4):
            t = part*4 + a
            total = acc[t] + pick(3, t, tsb)
            total = jnp.where(sub256 == ks_ref[t], total, 0.0)
            row = jnp.broadcast_to(jnp.sum(total, axis=0, keepdims=True), (8,256))
            row = jnp.where(sub < 4, row[:, :128], row[:, 128:])
            row = jnp.take_along_axis(row, spread, axis=1)
            chunk = jnp.where(lane // 32 == a, row, chunk)
        for x in range(XS):
            mine1[part, x] = chunk[2*x:2*x+2]
        for dx in range(XS):
            @pl.when((i < FEATS - 1) | (dx > 0))
            def _():
                to_share(i, dx, part, lax.rem(xpos + dx, XS), me).start()

    recv1[me] = mine1[feat, xpos]
    tests[ex] = tstage[xpos]
    for d, e in enumerate(epeers):
        to_tests(d, e, e).wait_recv()
    for df, dx, f, x in group:
        to_share((df + 7) % 8, dx, f, x, f*XS + x).wait_recv()
    entry = 2*xpos + lax.broadcasted_iota(jnp.int32, (2,128), 0)
    lines = []
    for x in range(XS):
        sk = jnp.zeros((2,128), jnp.float32)
        for f in range(FEATS):
            v = entry & f
            v = (v ^ (v >> 1) ^ (v >> 2)) & 1
            sk = sk + jnp.where(v == 1, -recv1[f*XS + x], recv1[f*XS + x])
        sk = sk * (float(67108864) ** -0.5)
        lines.append(jnp.concatenate([sk[0:1], sk[1:2]], axis=1))
    lhs = jnp.concatenate(lines*4, axis=0).astype(jnp.bfloat16)
    res = lax.dot_general(lhs, tests[...].reshape(1024, 256), (((1,), (1,)), ((), ())), preferred_element_type=jnp.float32)
    for x in range(XS):
        mine2[x] = res[x:x+1]
    for df, dx, f, x in group:
        to_score(df, dx, f, x, me).start()
    recv2[me] = mine2[xpos]
    for df, dx, f, x in group:
        to_score(df, dx, f, x, f*XS + x).wait_recv()
    total = recv2[0]
    for f in range(1, FEATS*XS):
        total = total + recv2[f]
    out_ref[...] = total
    for d, e in enumerate(epeers):
        to_tests(d, e, ex).wait_send()
    for df, dx, f, x in group:
        to_share((df + 7) % 8, dx, f, x, me).wait_send()
        to_score(df, dx, f, x, me).wait_send()

def scores_of(gradients, sign_words, sub_index, test_sketch):
    g = gradients.reshape(32, 4, 1, 65536)
    w = sign_words.reshape(32, 4, 32, 128)
    c = sub_index.reshape(8, 32, 32).transpose(1,0,2).reshape(32,1,256) & 65535
    kp = ((c >> 10) & 1)*128 + (c & 127)
    kq = c >> 11
    ks = (c >> 7) & 7
    col = np.arange(256)
    hh2 = (col >> 3) & 3
    h4 = jnp.asarray(hada(4)[:, hh2], jnp.float32)
    hm = jnp.asarray(k1_matrix(), jnp.bfloat16)
    hb = jnp.asarray(hada(256), jnp.bfloat16)
    anyspec = pl.BlockSpec(memory_space=pl.ANY)
    vm = pl.BlockSpec(memory_space=pltpu.VMEM)
    dma = pltpu.SemaphoreType.DMA
    return pl.pallas_call(
        kernel,
        out_shape=jax.ShapeDtypeStruct((1,1024), jnp.float32),
        in_specs=[anyspec, anyspec, vm, vm, vm, vm, vm, vm, anyspec],
        out_specs=vm,
        scratch_shapes=[
            pltpu.VMEM((NS, 32, 1, FB), jnp.bfloat16),
            pltpu.VMEM((4, 32, 32, 128), jnp.int32),
            pltpu.VMEM((32, 256, 256), jnp.bfloat16),
            pltpu.VMEM((32, 32, 256), jnp.float32),
            pltpu.VMEM((2*UNITS, 256, 128), jnp.bfloat16),
            pltpu.VMEM((2*UNITS, 256, 128), jnp.bfloat16),
            pltpu.VMEM((32, 2, 256, 128), jnp.bfloat16),
            pltpu.VMEM((32, 2, 256, 128), jnp.bfloat16),
            pltpu.VMEM((32, 8, 256), jnp.float32),
            pltpu.VMEM((XS, 64, 256), jnp.bfloat16),
            pltpu.VMEM((EXS, 64, 256), jnp.bfloat16),
            pltpu.VMEM((FEATS, XS, 2, 128), jnp.float32),
            pltpu.VMEM((FEATS*XS, 2, 128), jnp.float32),
            pltpu.VMEM((XS, 1, 1024), jnp.float32),
            pltpu.VMEM((FEATS*XS, 1, 1024), jnp.float32),
            dma((NS,)), dma((4,)), dma((8,)), dma((EXS - 1,)), dma((EXS,)),
            dma((FEATS*XS,)), dma((FEATS*XS,)), dma((FEATS*XS,)), dma((FEATS*XS,)),
        ],
        compiler_params=pltpu.CompilerParams(collective_id=0, has_side_effects=True, vmem_limit_bytes=60*1024*1024),
        cost_estimate=pl.CostEstimate(flops=17_000_000_000, bytes_accessed=36*1024*1024, transcendentals=0),
    )(g, w, kp, kq, ks, h4, hm, hb, test_sketch)

def on_device(gradients, sign_words, sub_index, test_sketch):
    return scores_of(gradients, sign_words, sub_index, test_sketch) * (8192.0 ** -0.5)

def solution(mesh):
    return jax.shard_map(on_device, mesh=mesh,
        in_specs=(P("ex", "feat"), P("feat"), P(), P("ex", None)),
        out_specs=P("ex", None), check_vma=False)
```

```python
import jax, jax.numpy as jnp, numpy as np
from jax import lax
from jax.experimental import pallas as pl
from jax.experimental.pallas import tpu as pltpu
from jax.sharding import PartitionSpec as P

def hada(n):
    h=np.ones((1,1))
    while h.shape[0]<n: h=np.block([[h,h],[h,-h]])
    return h

def k1_matrix():
    h32, h8 = hada(32), hada(8)
    rows = np.zeros((256,256))
    for j in range(16):
        for t in range(16):
            h5 = j + 16*(t//8); s = t%8
            rows[:, 16*j+t] = np.kron(h32[:,h5], h8[:,s])
    return rows

FB = 8192
NBLK = 32
NS = 12
UNITS = 4
TUNROLL = 4

FEATS, EXS, XS = 8, 16, 4
MESH = pl.DeviceIdType.MESH

def kernel(g_ref, w_ref, c_ref, h4_ref, hm_ref, hb_ref, t_ref, out_ref,
           raw, words, psel, sq, xs0, xs1, tsa, tsb, acc, tstage, tests, mine1, recv1, mine2, recv2, sem, wsem,
           tsem, send0, got0, send1, got1, send2, got2):
    feat = lax.axis_index("feat")
    ex = lax.axis_index("ex")
    xpos = lax.rem(ex, XS)
    zpos = ex // XS
    group = [(df, dx, lax.rem(feat + df, FEATS), lax.rem(xpos + dx, XS)) for df in range(FEATS) for dx in range(XS) if df or dx]
    epeers = [lax.rem(ex + d, EXS) for d in range(1, EXS)]
    far = [lax.rem(zpos + dz, EXS // XS)*XS + x for dz in range(1, EXS // XS) for x in range(XS)]
    me = feat*XS + xpos
    barrier = pltpu.get_barrier_semaphore()
    for _, _, f, x in group:
        pl.semaphore_signal(barrier, inc=1, device_id=(f, zpos*XS + x), device_id_type=MESH)
    for e in far:
        pl.semaphore_signal(barrier, inc=1, device_id=(feat, e), device_id_type=MESH)
    def tcopy(x, r):
        return pltpu.make_async_copy(t_ref.at[:, pl.ds(pl.multiple_of((2*x + r)*1024 + feat*128, 128), 128)],
            tstage.at[x, :, r*128:r*128+128], tsem.at[2*x + r])
    def remote(src, dst, send, got, f, e):
        return pltpu.make_async_remote_copy(src_ref=src, dst_ref=dst, send_sem=send, recv_sem=got,
            device_id=(f, e), device_id_type=MESH)
    def to_tests(d, e, slot):
        return remote(tstage.at[lax.rem(e, XS)], tests.at[slot], send0.at[d], got0.at[slot], feat, e)
    def to_share(i, dx, f, x, slot):
        return remote(mine1.at[f, x], recv1.at[slot], send1.at[i*XS + dx], got1.at[slot], f, zpos*XS + x)
    def to_score(df, dx, f, x, slot):
        return remote(mine2.at[x], recv2.at[slot], send2.at[df*XS + dx], got2.at[slot], f, zpos*XS + x)
    def gcopy(b):
        return pltpu.make_async_copy(g_ref.at[:, b // 8, :, pl.ds(pl.multiple_of((b % 8)*FB, FB), FB)], raw.at[b % NS], sem.at[b % NS])
    def wcopy(h2):
        return pltpu.make_async_copy(w_ref.at[:, h2], words.at[h2], wsem.at[h2])
    wcopy(0).start()
    for b in range(NS):
        gcopy(b).start()
    for h2 in range(1, 4):
        wcopy(h2).start()
    for x in range(XS):
        for r in range(2):
            tcopy(x, r).start()
    rows = lax.broadcasted_iota(jnp.int32, (256,256), 0)
    urow = lax.broadcasted_iota(jnp.int32, (32,256), 0)
    @pl.loop(0, 32//TUNROLL)
    def _(tt):
        for dt in range(TUNROLL):
            t = tt*TUNROLL + dt
            col = c_ref[t]
            onehot = jnp.where(rows == ((col >> 10) & 1)*128 + (col & 127), 1.0, 0.0).astype(jnp.bfloat16)
            psel[t] = jnp.dot(hb_ref[...], onehot, preferred_element_type=jnp.float32).astype(jnp.bfloat16)
            v = urow & (col >> 11)
            v = v ^ (v >> 4)
            v = v ^ (v >> 2)
            v = v ^ (v >> 1)
            sq[t] = jnp.where((v & 1) == 1, -1.0, 1.0)
    lane = lax.broadcasted_iota(jnp.int32, (8,128), 1)
    sub = lax.broadcasted_iota(jnp.int32, (8,128), 0)
    base = sub*8 + lane//16
    bit_lo = jnp.left_shift(1, lane % 16)
    bit_hi = jnp.left_shift(1, lane % 16 + 16)

    def prep(b, xs):
        slot = b % NS
        h2 = b // 8
        r0 = (b % 8)*UNITS
        for u in range(UNITS):
            for j in range(16):
                wlo = words[h2, j, pl.ds(r0 + u, 1), :]
                whi = words[h2, j+16, pl.ds(r0 + u, 1), :]
                wp = jnp.broadcast_to(wlo | (whi << 16), (8,128))
                for gam in range(2):
                    y = jnp.take_along_axis(wp, base + gam*64, axis=1)
                    parts = []
                    for hh, bit in ((j, bit_lo), (j+16, bit_hi)):
                        x = raw[slot, hh, :, u*2048 + gam*1024:u*2048 + gam*1024+1024]
                        x = x.astype(jnp.float32).reshape(8,128)
                        parts.append(jnp.where((y & bit) != 0, x, -x))
                    xs[2*u + gam, 16*j:16*j+16, :] = jnp.concatenate(parts, axis=0).astype(jnp.bfloat16)

    def mix(b, xs, ts):
        for pair in range(UNITS//2):
            outs = [jnp.dot(hm_ref[...], jnp.concatenate([xs[4*pair + 2*uu], xs[4*pair + 2*uu + 1]], axis=1), preferred_element_type=jnp.float32) for uu in range(2)]
            r0 = pl.multiple_of((b % 8)*(UNITS*8) + pair*16, 16)
            for t in range(32):
                for half in range(2):
                    c = half*128
                    ts[t, half, pl.ds(r0, 16), :] = jnp.concatenate([outs[0][8*t:8*t+8, c:c+128], outs[1][8*t:8*t+8, c:c+128]], axis=0).astype(jnp.bfloat16)

    def pick(h2, t, ts):
        u = jnp.dot(jnp.concatenate([ts[t, 0], ts[t, 1]], axis=1), psel[t], preferred_element_type=jnp.float32)
        tot = jnp.zeros((8,256), jnp.float32)
        for m in range(32):
            tot = tot + u[8*m:8*m+8] * jnp.broadcast_to(sq[t, m:m+1, :], (8,256))
        return tot * h4_ref[h2:h2+1, :]

    def arrive(b):
        @pl.when(b < NBLK)
        def _():
            gcopy(b).wait()
        @pl.when((b < NBLK) & (b % 8 == 0))
        def _():
            wcopy(b // 8).wait()
    def refill(b):
        @pl.when(b < NBLK)
        def _():
            gcopy(b).start()

    arrive(0)
    prep(0, xs0)
    refill(NS)
    for h2 in range(4):
        new, old = (tsa, tsb) if h2 % 2 == 0 else (tsb, tsa)
        @pl.loop(0, 4)
        def _(i):
            b = 8*h2 + 2*i
            if h2 == 0:
                @pl.when(i == 3)
                def _():
                    pl.semaphore_wait(barrier, len(group) + len(far))
                    for x in range(XS):
                        for r in range(2):
                            tcopy(x, r).wait()
                    for d, e in enumerate(epeers):
                        to_tests(d, e, ex).start()
            arrive(b + 1)
            arrive(b + 2)
            for k, (xa, xb) in enumerate(((xs1, xs0), (xs0, xs1))):
                prep(jnp.minimum(b + k + 1, NBLK - 1), xa)
                mix(b + k, xb, new)
                if h2 > 0:
                    for dt in range(4):
                        t = 8*i + 4*k + dt
                        val = pick(h2 - 1, t, old)
                        acc[t] = val if h2 == 1 else acc[t] + val
            refill(b + 1 + NS)
            refill(b + 2 + NS)

    sub256 = lax.broadcasted_iota(jnp.int32, (8,256), 0)
    spread = (sub % 4)*32 + lane % 32
    @pl.loop(0, 8)
    def _(i):
        part = lax.rem(feat + 1 + i, FEATS)
        chunk = jnp.zeros((8,128), jnp.float32)
        for a in range(4):
            t = part*4 + a
            total = acc[t] + pick(3, t, tsb)
            total = jnp.where(sub256 == ((c_ref[t] >> 7) & 7), total, 0.0)
            row = jnp.broadcast_to(jnp.sum(total, axis=0, keepdims=True), (8,256))
            row = jnp.where(sub < 4, row[:, :128], row[:, 128:])
            row = jnp.take_along_axis(row, spread, axis=1)
            chunk = jnp.where(lane // 32 == a, row, chunk)
        for x in range(XS):
            mine1[part, x] = chunk[2*x:2*x+2]
        for dx in range(XS):
            @pl.when((i < FEATS - 1) | (dx > 0))
            def _():
                to_share(i, dx, part, lax.rem(xpos + dx, XS), me).start()

    recv1[me] = mine1[feat, xpos]
    tests[ex] = tstage[xpos]
    for d, e in enumerate(epeers):
        to_tests(d, e, e).wait_recv()
    for df, dx, f, x in group:
        to_share((df + 7) % 8, dx, f, x, f*XS + x).wait_recv()
    entry = 2*xpos + lax.broadcasted_iota(jnp.int32, (2,128), 0)
    lines = []
    for x in range(XS):
        sk = jnp.zeros((2,128), jnp.float32)
        for f in range(FEATS):
            v = entry & f
            v = (v ^ (v >> 1) ^ (v >> 2)) & 1
            sk = sk + jnp.where(v == 1, -recv1[f*XS + x], recv1[f*XS + x])
        sk = sk * (float(67108864) ** -0.5)
        lines.append(jnp.concatenate([sk[0:1], sk[1:2]], axis=1))
    lhs = jnp.concatenate(lines*4, axis=0).astype(jnp.bfloat16)
    res = lax.dot_general(lhs, tests[...].reshape(1024, 256), (((1,), (1,)), ((), ())), preferred_element_type=jnp.float32)
    for x in range(XS):
        mine2[x] = res[x:x+1]
    for df, dx, f, x in group:
        to_score(df, dx, f, x, me).start()
    recv2[me] = mine2[xpos]
    for df, dx, f, x in group:
        to_score(df, dx, f, x, f*XS + x).wait_recv()
    total = recv2[0]
    for f in range(1, FEATS*XS):
        total = total + recv2[f]
    out_ref[...] = total
    for d, e in enumerate(epeers):
        to_tests(d, e, ex).wait_send()
    for df, dx, f, x in group:
        to_share((df + 7) % 8, dx, f, x, me).wait_send()
        to_score(df, dx, f, x, me).wait_send()

def scores_of(gradients, sign_words, sub_index, test_sketch):
    g = gradients.reshape(32, 4, 1, 65536)
    w = sign_words.reshape(32, 4, 32, 128)
    c = sub_index.reshape(8, 32, 32).transpose(1,0,2).reshape(32,1,256) & 65535
    col = np.arange(256)
    hh2 = (col >> 3) & 3
    h4 = jnp.asarray(hada(4)[:, hh2], jnp.float32)
    hm = jnp.asarray(k1_matrix(), jnp.bfloat16)
    hb = jnp.asarray(hada(256), jnp.bfloat16)
    anyspec = pl.BlockSpec(memory_space=pl.ANY)
    vm = pl.BlockSpec(memory_space=pltpu.VMEM)
    dma = pltpu.SemaphoreType.DMA
    return pl.pallas_call(
        kernel,
        out_shape=jax.ShapeDtypeStruct((1,1024), jnp.float32),
        in_specs=[anyspec, anyspec, vm, vm, vm, vm, anyspec],
        out_specs=vm,
        scratch_shapes=[
            pltpu.VMEM((NS, 32, 1, FB), jnp.bfloat16),
            pltpu.VMEM((4, 32, 32, 128), jnp.int32),
            pltpu.VMEM((32, 256, 256), jnp.bfloat16),
            pltpu.VMEM((32, 32, 256), jnp.float32),
            pltpu.VMEM((2*UNITS, 256, 128), jnp.bfloat16),
            pltpu.VMEM((2*UNITS, 256, 128), jnp.bfloat16),
            pltpu.VMEM((32, 2, 256, 128), jnp.bfloat16),
            pltpu.VMEM((32, 2, 256, 128), jnp.bfloat16),
            pltpu.VMEM((32, 8, 256), jnp.float32),
            pltpu.VMEM((XS, 64, 256), jnp.bfloat16),
            pltpu.VMEM((EXS, 64, 256), jnp.bfloat16),
            pltpu.VMEM((FEATS, XS, 2, 128), jnp.float32),
            pltpu.VMEM((FEATS*XS, 2, 128), jnp.float32),
            pltpu.VMEM((XS, 1, 1024), jnp.float32),
            pltpu.VMEM((FEATS*XS, 1, 1024), jnp.float32),
            dma((NS,)), dma((4,)), dma((8,)), dma((EXS - 1,)), dma((EXS,)),
            dma((FEATS*XS,)), dma((FEATS*XS,)), dma((FEATS*XS,)), dma((FEATS*XS,)),
        ],
        compiler_params=pltpu.CompilerParams(collective_id=0, has_side_effects=True, vmem_limit_bytes=60*1024*1024),
        cost_estimate=pl.CostEstimate(flops=17_000_000_000, bytes_accessed=36*1024*1024, transcendentals=0),
    )(g, w, c, h4, hm, hb, test_sketch)

def on_device(gradients, sign_words, sub_index, test_sketch):
    return scores_of(gradients, sign_words, sub_index, test_sketch) * (8192.0 ** -0.5)

def solution(mesh):
    return jax.shard_map(on_device, mesh=mesh,
        in_specs=(P("ex", "feat"), P("feat"), P(), P("ex", None)),
        out_specs=P("ex", None), check_vma=False)
```
